32 devices in a mesh: groups: 2 (over x), shot: 16 (over z, y, core).
Axes of the slice: x: 2, y: 2, z: 4, core: 2. Of those that a mesh axis runs over, the one named last changes fastest.
Arguments:
- velocity: float32 [64, 4, 64, 128], P(('groups', 'shot')), parts along dimension 0, may hold values from 1.5 to 4
- tile_owner: int32 [32], replicated, may hold values from 0 to 15, as said below
- aperture: int32 [32, 16], P(('groups', 'shot')), parts along dimension 0, may hold values from 0 to 31, as said below
- source_at: int32 [32, 256], P(('groups', 'shot')), parts along dimension 0, may hold values from 0 to 524287
- source_amp: float32 [32, 256], P(('groups', 'shot')), parts along dimension 0, may hold values from -6 to 6
- receivers: int32 [32, 128], P(('groups', 'shot')), parts along dimension 0, may hold values from 0 to 524287
- wavelet: float32 [16], replicated, may hold values from -4 to 4
- observed: float32 [32, 16, 128], P(('groups', 'shot')), parts along dimension 0, may hold values from -6 to 6
Outputs:
- gradient: float32 [64, 4, 64, 128], P(('groups', 'shot')), parts along dimension 0
- misfit: float32 [32, 16, 128], P(('groups', 'shot')), parts along dimension 0
The draws below stay inside these ranges and needn't reach their ends.
There are 2 independent parts, one for each index of `groups`. The reference program is written for one: setup_inputs(seed, part) draws one part's arguments, and reference() takes and returns one part's arrays. A program takes and returns all parts, laid end to end along the dimension named above; an argument that names none is the same for every part. Nothing has to cross between parts.
Inputs may be any that keep to these rules, and one draw needn't show every extreme that they name: tile_owner[t] depends only on t % 16, and distinct residues have distinct owners. `aperture`: each row holds 16 consecutive slab numbers in rising order.
All inputs are finite; a program needn't handle non-finite values.
Results may differ from the reference program's by a relative error of at most 0.0003.
Values sent between devices are 32-bit elements; how exact they have to be, the bound alone decides.
No kernel may reach another device: no remote copies, remote signals or barrier semaphores. Data moves between devices by JAX's collectives and lax.ppermute only.
A program may use at most 256 MiB of HBM per device.

```python
import jax
import jax.numpy as jnp
from jax import lax

TX = 4
NY = 64
NZ = 128
APER = 16
NSTEP = 16
NSRC = 256
NREC = 128
SHOTS = 16
NTILES = 32
N_SHOT = 16


def draw_tile_owner(key, part):
    key = jax.random.fold_in(key, 11)
    order = jax.random.permutation(key, N_SHOT).astype(jnp.int32)
    return order[jnp.arange(NTILES, dtype=jnp.int32) % N_SHOT]


def draw_aperture(key, part):
    key = jax.random.fold_in(key, 23)
    first_key, pick_key = jax.random.split(key)
    starts = jax.random.randint(first_key, (SHOTS,), 0, NTILES - APER + 1).astype(jnp.int32)
    chosen = jax.random.randint(pick_key, (), 0, SHOTS).astype(jnp.int32)
    starts = starts.at[chosen].set(0)
    starts = starts.at[(chosen + 1) % SHOTS].set(NTILES - APER)
    return (starts[:, None] + jnp.arange(APER, dtype=jnp.int32)[None, :]).astype(jnp.int32)


def touch_ends(result, rng, least, high):
    extent = result.shape
    index_at = [jax.random.randint(jax.random.fold_in(rng, axis), (), 0, extent[axis]) for axis in range(len(extent))]
    result = result.at[tuple(index_at)].set(least)
    longest = extent.index(max(extent))
    index_at[longest] = (index_at[longest] + 1) % extent[longest]
    return result.at[tuple(index_at)].set(high)


def block_levels(key, shape, cuts, smallest, top_value):
    factor_of = 1.0
    for axis_at, shards_of in cuts:
        steps = jax.random.uniform(jax.random.fold_in(jax.random.fold_in(key, 6), axis_at), (shards_of,), jnp.float32, smallest / len(cuts), top_value / len(cuts))
        factor_of = factor_of * jnp.repeat(jnp.exp(steps), shape[axis_at] // shards_of).reshape((-1,) + (1,) * (len(shape) - 1 - axis_at))
    return factor_of


def normal_values(rng, dims, scale, limit, cuts=(), kind=jnp.bfloat16):
    entries = scale * jax.random.normal(rng, dims, jnp.float32)
    if cuts:
        entries = entries * block_levels(rng, dims, cuts, -0.22, 0.18)
    return jnp.clip(entries, -limit, limit).astype(kind)


def setup_inputs(seed: int = 0, part: int = 0) -> dict:
    key_of = jax.random.split(jax.random.key(seed), 9)
    own_keys = jax.random.split(jax.random.fold_in(key_of[8], part), 9)
    velocity = jnp.clip(1.5 + 2.5 * jax.random.uniform(own_keys[0], (NTILES, TX, NY, NZ), jnp.float32) ** block_levels(own_keys[0], (NTILES, TX, NY, NZ), ((0, 16),), -0.2, 0.2), 1.5, 4.0)
    tile_owner = draw_tile_owner(jax.random.fold_in(key_of[8], 71), part)
    aperture = draw_aperture(jax.random.fold_in(jax.random.fold_in(key_of[8], part), 71), part)
    source_at = touch_ends(jax.random.randint(own_keys[3], (SHOTS, NSRC), 0, APER * TX * NY * NZ), jax.random.fold_in(own_keys[3], 1), 0, (APER * TX * NY * NZ) - 1).astype(jnp.int32)
    source_amp = normal_values(own_keys[4], (SHOTS, NSRC), 1.0, 6.0, ((0, 16),), jnp.float32)
    receivers = touch_ends(jax.random.randint(own_keys[5], (SHOTS, NREC), 0, APER * TX * NY * NZ), jax.random.fold_in(own_keys[5], 1), 0, (APER * TX * NY * NZ) - 1).astype(jnp.int32)
    wavelet = normal_values(key_of[6], (NSTEP,), 1.0, 4.0, (), jnp.float32)
    observed = normal_values(own_keys[7], (SHOTS, NSTEP, NREC), 1.0, 6.0, ((0, 16),), jnp.float32)
    return {"velocity": velocity, "tile_owner": tile_owner, "aperture": aperture, "source_at": source_at, "source_amp": source_amp, "receivers": receivers, "wavelet": wavelet, "observed": observed}


COEF = (-205.0 / 72.0, 1.6, -0.2, 8.0 / 315.0, -1.0 / 560.0)
STEP_RATIO = 0.1


def laplace(field):
    padded = jnp.pad(field, 4)
    size_x, size_y, size_z = field.shape
    total = (3.0 * COEF[0]) * field
    for k in range(1, 5):
        total = total + COEF[k] * (padded[4 + k:4 + k + size_x, 4:4 + size_y, 4:4 + size_z] + padded[4 - k:4 - k + size_x, 4:4 + size_y, 4:4 + size_z])
        total = total + COEF[k] * (padded[4:4 + size_x, 4 + k:4 + k + size_y, 4:4 + size_z] + padded[4:4 + size_x, 4 - k:4 - k + size_y, 4:4 + size_z])
        total = total + COEF[k] * (padded[4:4 + size_x, 4:4 + size_y, 4 + k:4 + k + size_z] + padded[4:4 + size_x, 4:4 + size_y, 4 - k:4 - k + size_z])
    return total


def propagate(region, spots, amps, wavelet, listeners, recorded):
    shape = region.shape
    speed2 = (STEP_RATIO * region) ** 2
    zeros = jnp.zeros(shape, jnp.float32)

    def inject(field, where, values):
        return field.reshape(-1).at[where].add(values).reshape(shape)

    fields = [zeros]
    before = zeros
    current = zeros
    records = []
    for step in range(wavelet.shape[0]):
        nxt = 2.0 * current - before + speed2 * laplace(current)
        nxt = inject(nxt, spots, amps * wavelet[step])
        records.append(nxt.reshape(-1)[listeners])
        before, current = current, nxt
        fields.append(nxt)
    misfit = jnp.stack(records) - recorded
    after = zeros
    current = zeros
    image = zeros
    for step in range(wavelet.shape[0] - 1, -1, -1):
        nxt = 2.0 * current - after + speed2 * laplace(current)
        nxt = inject(nxt, listeners, misfit[step])
        after, current = current, nxt
        if step >= 1:
            image = image + nxt * (fields[step + 1] - 2.0 * fields[step] + fields[step - 1])
    return misfit, (2.0 / region) * image


def reference(velocity, tile_owner, aperture, source_at, source_amp, receivers, wavelet, observed):
    per_dev = velocity.shape[0] // N_SHOT
    store_row = (tile_owner * per_dev + jnp.arange(velocity.shape[0], dtype=jnp.int32) // N_SHOT).astype(jnp.int32)
    cell_shape = velocity.shape[1:]

    def one_shot(total, inputs):
        slabs, spots, amps, listeners, recorded = inputs
        rows = store_row[slabs]
        region = velocity[rows].reshape((-1,) + cell_shape[1:])
        misfit, shot_grad = propagate(region, spots, amps, wavelet, listeners, recorded)
        total = total.at[rows].add(shot_grad.reshape((slabs.shape[0],) + cell_shape))
        return total, misfit

    start = jnp.zeros(velocity.shape, jnp.float32)
    gradient, misfit = lax.scan(one_shot, start, (aperture, source_at, source_amp, receivers, observed))
    return gradient, misfit
```

```python
import jax
import jax.numpy as jnp
import numpy as np
from jax import lax
from jax.experimental import pallas as pl
from jax.experimental.pallas import tpu as pltpu
from jax.sharding import PartitionSpec as P

STEP_RATIO = 0.1
TAPS = (63.0, -7.875, 1.0, -0.0703125)
CENTER_Z = -336.0
CENTER_Y = -0.328125
SCALE = 128.0 / 5040.0
REACH = 4
LANES = 128
GROUP = 4


def band(size, center):
    out = np.zeros((size, size), np.float32)
    np.fill_diagonal(out, center)
    for k, tap in enumerate(TAPS, 1):
        at = np.arange(size - k)
        out[at, at + k] = tap
        out[at + k, at] = tap
    return out


def kernel(
    rows_ref, slot_ref, rec_ref, wav_ref,
    vel_ref, src_hbm, pick_ref, same_ref, obs_ref, mat_y_ref, mat_z_ref,
    grad_ref, mis_ref,
    hist, field, halves, speed, region, dense, rate, rec_rows, moved, in_sem, src_sem, out_sem,
):
    nstep, cells, _ = hist.shape
    nrec = pick_ref.shape[0]
    ny = mat_y_ref.shape[0] // 2
    slab = vel_ref.shape[1]
    edge = REACH * ny
    block = GROUP * ny
    groups = cells // block
    held = slot_ref.shape[0]

    def fetch(j):
        return pltpu.make_async_copy(
            vel_ref.at[rows_ref[j]], region.at[pl.ds(j * slab, slab), :], in_sem.at[j]
        )

    def blank(r):
        return pltpu.make_async_copy(field.at[0, pl.ds(0, slab), :], grad_ref.at[r], out_sem.at[r])

    def give(r):
        at = pl.multiple_of(jnp.maximum(slot_ref[r], 0) * slab, slab)
        return pltpu.make_async_copy(dense.at[pl.ds(at, slab), :], grad_ref.at[r], out_sem.at[r])

    source = pltpu.make_async_copy(src_hbm, dense, src_sem)
    source.start()
    for j in range(rows_ref.shape[0]):
        fetch(j).start()

    zeros = jnp.zeros((edge, LANES), jnp.float32)
    for b in range(2):
        field[b, 0:edge, :] = zeros
        field[b, edge + cells : edge + cells + edge, :] = zeros

    for r in range(held):
        @pl.when(slot_ref[r] < 0)
        def _():
            blank(r).start()

    def keep(at, value):
        high = value.astype(jnp.bfloat16)
        halves[pl.ds(at, 16), 0:LANES] = high
        halves[pl.ds(at, 16), LANES : 2 * LANES] = (value - high.astype(jnp.float32)).astype(jnp.bfloat16)

    def listen(n, b):
        def body(r, _):
            rec_rows[n, pl.ds(r, 1), :] = field[b, pl.ds(edge + rec_ref[r], 1), :]
            return 0

        lax.fori_loop(0, nrec, body, 0, unroll=16)

    def sweep(cur, update):
        def body(g, _):
            base = pl.multiple_of(g * block, block)
            both = halves[pl.ds(base, block), :]
            along_z = jnp.dot(both, mat_z_ref[...], preferred_element_type=jnp.float32)
            plane = [both[i * ny : (i + 1) * ny] for i in range(GROUP)]
            cols = []
            for i in range(0, GROUP, 2):
                cols.append(
                    jnp.concatenate(
                        [plane[i][:, :LANES], plane[i][:, LANES:], plane[i + 1][:, :LANES], plane[i + 1][:, LANES:]],
                        axis=0,
                    )
                )
            along_y = jnp.dot(
                mat_y_ref[...], jnp.concatenate(cols, axis=1), preferred_element_type=jnp.float32
            )
            for j in range(0, ny, 16):
                near = [
                    field[cur, pl.ds(base + d * ny + j, 16), :] for d in range(GROUP + 2 * REACH)
                ]
                for i in range(GROUP):
                    lap = near[i + 4 - 3] + near[i + 4 + 3]
                    lap = lap + TAPS[0] * (near[i + 4 - 1] + near[i + 4 + 1])
                    lap = lap + TAPS[1] * (near[i + 4 - 2] + near[i + 4 + 2])
                    lap = lap + TAPS[3] * (near[i + 4 - 4] + near[i + 4 + 4])
                    lap = lap + along_z[i * ny + j : i * ny + j + 16]
                    at_y = (i % 2) * ny + j
                    lap = lap + along_y[at_y : at_y + 16, (i // 2) * LANES : (i // 2 + 1) * LANES]
                    at = pl.multiple_of(base + i * ny + j, 16)
                    update(at, near[i + 4], lap)
            return 0

        lax.fori_loop(0, groups, body, 0)

    def rows16(fn):
        def body(g, _):
            fn(pl.multiple_of(g * 16, 16))
            return 0

        lax.fori_loop(0, cells // 16, body, 0, unroll=4)

    source.wait()

    def first(at):
        value = wav_ref[0] * dense[pl.ds(at, 16), :]
        hist[0, pl.ds(at, 16), :] = value
        field[0, pl.ds(edge + at, 16), :] = value
        keep(at, value)

    rows16(first)
    listen(0, 0)

    for j in range(rows_ref.shape[0]):
        fetch(j).wait()

    def squared(at):
        scaled = STEP_RATIO * region[pl.ds(at, 16), :]
        speed[pl.ds(at, 16), :] = (scaled * scaled) * SCALE

    rows16(squared)

    def forward(n, _):
        cur = (n - 1) & 1
        new = n & 1
        strength = wav_ref[n]

        def update(at, here, lap):
            here_rate = hist[n - 1, pl.ds(at, 16), :] + (
                speed[pl.ds(at, 16), :] * lap + strength * dense[pl.ds(at, 16), :]
            )
            value = here + here_rate
            hist[n, pl.ds(at, 16), :] = here_rate
            field[new, pl.ds(edge + at, 16), :] = value
            keep(at, value)

        sweep(cur, update)
        listen(n, new)
        return 0

    lax.fori_loop(1, nstep, forward, 0)

    step_lane = lax.broadcasted_iota(jnp.int32, (nrec, nstep), 1)

    def compare(n, total):
        picked = jnp.sum(rec_rows[n] * pick_ref[...], axis=1, keepdims=True)
        total = jnp.where(step_lane == n, picked, total)
        seen = jnp.sum(jnp.where(step_lane == n, obs_ref[...], 0.0), axis=1, keepdims=True)
        rec_rows[n] = jnp.dot(
            same_ref[...], pick_ref[...] * (picked - seen),
            preferred_element_type=jnp.float32, precision=lax.Precision.HIGHEST,
        )
        return total

    records = lax.fori_loop(0, nstep, compare, jnp.zeros((nrec, nstep), jnp.float32))
    mis_ref[...] = records - obs_ref[...]

    def inject(n):
        def take(r, _):
            moved[pl.ds(r, 1), :] = rate[pl.ds(rec_ref[r], 1), :]
            return 0

        lax.fori_loop(0, nrec, take, 0, unroll=16)
        moved[...] = moved[...] + rec_rows[n]

        def put(r, _):
            rate[pl.ds(rec_ref[r], 1), :] = moved[pl.ds(r, 1), :]
            return 0

        lax.fori_loop(0, nrec, put, 0, unroll=16)

    def clear(at):
        rate[pl.ds(at, 16), :] = jnp.zeros((16, LANES), jnp.float32)

    rows16(clear)
    inject(nstep - 1)

    def last(at):
        value = rate[pl.ds(at, 16), :]
        field[(nstep - 1) & 1, pl.ds(edge + at, 16), :] = value
        dense[pl.ds(at, 16), :] = hist[nstep - 1, pl.ds(at, 16), :] * value
        keep(at, value)

    rows16(last)

    def backward(k, _):
        n = nstep - 1 - k
        inject(n - 1)

        def update(at, here, lap):
            here_rate = rate[pl.ds(at, 16), :] + speed[pl.ds(at, 16), :] * lap
            value = here + here_rate
            rate[pl.ds(at, 16), :] = here_rate
            field[(n - 1) & 1, pl.ds(edge + at, 16), :] = value
            dense[pl.ds(at, 16), :] = dense[pl.ds(at, 16), :] + hist[n - 1, pl.ds(at, 16), :] * here_rate
            keep(at, value)

        sweep(n & 1, update)
        return 0

    lax.fori_loop(0, nstep - 2, backward, 0)

    def finish(at):
        image = dense[pl.ds(at, 16), :] - hist[0, pl.ds(at, 16), :] * field[1, pl.ds(edge + at, 16), :]
        dense[pl.ds(at, 16), :] = (2.0 / region[pl.ds(at, 16), :]) * image

    rows16(finish)

    for r in range(held):
        @pl.when(slot_ref[r] >= 0)
        def _():
            give(r).start()

    for r in range(held):
        blank(r).wait()


def shot(store_rows, slots, rec_at, wavelet, pieces, sources, picks, same, observed):
    held, slab = pieces.shape[0], pieces.shape[1] * pieces.shape[2]
    ny, nz = pieces.shape[2:]
    aper = store_rows.shape[0]
    cells = aper * slab
    nstep, nrec = wavelet.shape[0], rec_at.shape[0]
    in_y = band(ny, CENTER_Y)
    none = np.zeros_like(in_y)
    mat_y = np.block([[in_y, in_y, none, none], [none, none, in_y, in_y]])
    in_z = band(nz, CENTER_Z)
    mat_z = np.concatenate([in_z, in_z], axis=0)
    smem = pl.BlockSpec(memory_space=pltpu.SMEM)
    vmem = pl.BlockSpec(memory_space=pltpu.VMEM)
    hbm = pl.BlockSpec(memory_space=pl.ANY)
    f32 = jnp.float32
    edge = REACH * ny
    grad, misfit = pl.pallas_call(
        kernel,
        out_shape=(
            jax.ShapeDtypeStruct((held, slab, nz), f32),
            jax.ShapeDtypeStruct((nrec, nstep), f32),
        ),
        in_specs=[smem] * 4 + [hbm] * 2 + [vmem] * 5,
        out_specs=(hbm, vmem),
        scratch_shapes=[
            pltpu.VMEM((nstep, cells, nz), f32),
            pltpu.VMEM((2, cells + 2 * edge, nz), f32),
            pltpu.VMEM((cells, 2 * nz), jnp.bfloat16),
            pltpu.VMEM((cells, nz), f32),
            pltpu.VMEM((cells, nz), f32),
            pltpu.VMEM((cells, nz), f32),
            pltpu.VMEM((cells, nz), f32),
            pltpu.VMEM((nstep, nrec, nz), f32),
            pltpu.VMEM((nrec, nz), f32),
            pltpu.SemaphoreType.DMA((aper,)),
            pltpu.SemaphoreType.DMA,
            pltpu.SemaphoreType.DMA((held,)),
        ],
        compiler_params=pltpu.CompilerParams(vmem_limit_bytes=60 * 1024 * 1024),
        name="shot_gradient",
    )(
        store_rows, slots, rec_at, wavelet,
        pieces.reshape(held, slab, nz), sources, picks, same, observed,
        jnp.asarray(mat_y, jnp.bfloat16), jnp.asarray(mat_z, jnp.bfloat16),
    )
    return grad.reshape(pieces.shape), misfit


def shards(velocity, tile_owner, aperture, source_at, source_amp, receivers, wavelet, observed):
    devices = lax.axis_size("shot")
    per_dev = velocity.shape[0]
    slabs = aperture[0]
    store_rows = tile_owner[slabs] * per_dev + slabs // devices
    pieces = lax.all_gather(velocity, "shot", axis=0, tiled=True)
    held = pieces.shape[0]
    nz = velocity.shape[3]
    hit = jnp.arange(held, dtype=jnp.int32)[:, None] == store_rows[None, :]
    slots = jnp.max(jnp.where(hit, jnp.arange(slabs.shape[0], dtype=jnp.int32)[None, :], -1), axis=1)
    cells = slabs.shape[0] * velocity.shape[1] * velocity.shape[2]
    sources = jnp.zeros((cells * nz,), jnp.float32).at[source_at[0]].add(source_amp[0]).reshape(cells, nz)
    rec_at = receivers[0] // nz
    lane = receivers[0] % nz
    picks = (lane[:, None] == jnp.arange(nz, dtype=jnp.int32)[None, :]).astype(jnp.float32)
    same = (rec_at[:, None] == rec_at[None, :]).astype(jnp.float32)
    grad, misfit = shot(store_rows, slots, rec_at, wavelet, pieces, sources, picks, same, observed[0].T)
    gradient = lax.psum_scatter(grad, "shot", scatter_dimension=0, tiled=True)
    return (gradient, misfit.T[None])


def solution(mesh):
    in_specs = (
        P(("groups", "shot"), None, None, None),
        P(),
        P(("groups", "shot"), None),
        P(("groups", "shot"), None),
        P(("groups", "shot"), None),
        P(("groups", "shot"), None),
        P(),
        P(("groups", "shot"), None, None),
    )
    out_specs = (P(("groups", "shot"), None, None, None), P(("groups", "shot"), None, None))
    return jax.shard_map(shards, mesh=mesh, in_specs=in_specs, out_specs=out_specs, check_vma=False)
```

```python
import functools

import jax
import jax.numpy as jnp
import numpy as np
from jax import lax
from jax.experimental import pallas as pl
from jax.experimental.pallas import tpu as pltpu
from jax.sharding import PartitionSpec as P

STEP_RATIO = 0.1
TAPS = (63.0, -7.875, 1.0, -0.0703125)
CENTER_Z = -336.0
CENTER_Y = -0.328125
SCALE = 128.0 / 5040.0
REACH = 4
LANES = 128
GROUP = 8


def band(size, center):
    out = np.zeros((size, size), np.float32)
    np.fill_diagonal(out, center)
    for k, tap in enumerate(TAPS, 1):
        at = np.arange(size - k)
        out[at, at + k] = tap
        out[at + k, at] = tap
    return out


def kernel(
    sources, targets, take_ref, give_ref, rec_ref, wav_ref, src_hbm, pick_ref, same_ref, obs_ref, mat_y_ref, mat_z_ref,
    *refs,
):
    vel_refs, refs = refs[:sources], refs[sources:]
    grad_refs, refs = refs[:targets], refs[targets:]
    (
        mis_ref, hist_a, hist_b, field_a, field_b, halves_a, halves_b, taps_a, taps_b,
        speed, region, dense, rate, rec_rows, moved, in_sem, src_sem, out_sem,
    ) = refs
    nstep = wav_ref.shape[0]
    cells = speed.shape[0]
    nrec = pick_ref.shape[0]
    ny = mat_y_ref.shape[0] // 2
    per, slab = vel_refs[0].shape[:2]
    out_per = grad_refs[0].shape[0]
    aper = cells // slab
    edge = REACH * ny
    block = GROUP * ny
    groups = cells // block
    held = give_ref.shape[0]

    def fetch(i, j):
        at = pl.multiple_of(j * slab, slab)
        return pltpu.make_async_copy(
            vel_refs[i // per].at[i % per], region.at[pl.ds(at, slab), :], in_sem.at[j]
        )

    def blank(r):
        return pltpu.make_async_copy(
            field_a.at[pl.ds(0, slab), :], grad_refs[r // out_per].at[r % out_per], out_sem.at[r]
        )

    def give(r):
        at = pl.multiple_of(give_ref[r] * slab, slab)
        return pltpu.make_async_copy(
            dense.at[pl.ds(at, slab), :], grad_refs[r // out_per].at[r % out_per], out_sem.at[r]
        )

    source = pltpu.make_async_copy(src_hbm, dense, src_sem)
    source.start()
    for i in range(sources * per):
        @pl.when(take_ref[i] >= 0)
        def _():
            fetch(i, take_ref[i]).start()

    zeros = jnp.zeros((edge, LANES), jnp.float32)
    for field in (field_a, field_b):
        field[0:edge, :] = zeros
        field[edge + cells : edge + cells + edge, :] = zeros

    for r in range(held):
        @pl.when(give_ref[r] < 0)
        def _():
            blank(r).start()

    fields = (field_a, field_b)
    hist = (hist_a, hist_b)
    halves = (halves_a, halves_b)

    def keep(to, at, value):
        high = value.astype(jnp.bfloat16)
        halves[to][pl.ds(at, 16), 0:LANES] = high
        halves[to][pl.ds(at, 16), LANES : 2 * LANES] = (value - high.astype(jnp.float32)).astype(jnp.bfloat16)

    def listen(n, to):
        def body(r, _):
            rec_rows[n, pl.ds(r, 1), :] = fields[to][pl.ds(edge + rec_ref[r], 1), :]
            return 0

        lax.fori_loop(0, nrec, body, 0, unroll=16)

    def multiply(base, of, taps):
        both = halves[of][pl.ds(base, block), :]
        along_z = jnp.dot(both, mat_z_ref[...], preferred_element_type=jnp.float32)
        plane = [both[i * ny : (i + 1) * ny] for i in range(GROUP)]
        cols = []
        for i in range(0, GROUP, 2):
            cols.append(
                jnp.concatenate(
                    [plane[i][:, :LANES], plane[i][:, LANES:], plane[i + 1][:, :LANES], plane[i + 1][:, LANES:]],
                    axis=0,
                )
            )
        along_y = jnp.dot(mat_y_ref[...], jnp.concatenate(cols, axis=1), preferred_element_type=jnp.float32)
        for i in range(GROUP):
            taps[i * ny : (i + 1) * ny, :] = (
                along_z[i * ny : (i + 1) * ny]
                + along_y[(i % 2) * ny : (i % 2 + 1) * ny, (i // 2) * LANES : (i // 2 + 1) * LANES]
            )

    def combine(base, of, taps, update):
        for j in range(0, ny, 16):
            near = [fields[of][pl.ds(base + d * ny + j, 16), :] for d in range(GROUP + 2 * REACH)]
            for i in range(GROUP):
                lap = near[i + 4 - 3] + near[i + 4 + 3]
                lap = lap + TAPS[0] * (near[i + 4 - 1] + near[i + 4 + 1])
                lap = lap + TAPS[1] * (near[i + 4 - 2] + near[i + 4 + 2])
                lap = lap + TAPS[3] * (near[i + 4 - 4] + near[i + 4 + 4])
                lap = lap + taps[i * ny + j : i * ny + j + 16, :]
                at = base + i * ny + j
                update(at if isinstance(at, int) else pl.multiple_of(at, 16), near[i + 4], lap)

    def sweep(of, update):
        def body(g, _):
            base = pl.multiple_of(g * (2 * block), 2 * block)
            multiply(base + block, of, taps_b)
            combine(base, of, taps_a, update)
            multiply(base + 2 * block, of, taps_a)
            combine(base + block, of, taps_b, update)
            return 0

        lax.fori_loop(0, groups // 2 - 1, body, 0)
        base = (groups - 2) * block
        multiply(base + block, of, taps_b)
        combine(base, of, taps_a, update)
        multiply(0, 1 - of, taps_a)
        combine(base + block, of, taps_b, update)

    def rows16(fn):
        def body(g, _):
            fn(pl.multiple_of(g * 16, 16))
            return 0

        lax.fori_loop(0, cells // 16, body, 0, unroll=4)

    source.wait()

    def first(at):
        value = wav_ref[0] * dense[pl.ds(at, 16), :]
        hist_a[0, pl.ds(at, 16), :] = value
        field_a[pl.ds(edge + at, 16), :] = value
        keep(0, at, value)

    rows16(first)
    multiply(0, 0, taps_a)
    listen(0, 0)

    for j in range(aper):
        fetch(0, j).wait()

    def squared(at):
        scaled = STEP_RATIO * region[pl.ds(at, 16), :]
        speed[pl.ds(at, 16), :] = (scaled * scaled) * SCALE

    rows16(squared)

    def forward(n, of):
        strength = wav_ref[n]

        def update(at, here, lap):
            here_rate = hist[of][(n - 1) // 2, pl.ds(at, 16), :] + (
                speed[pl.ds(at, 16), :] * lap + strength * dense[pl.ds(at, 16), :]
            )
            value = here + here_rate
            hist[1 - of][n // 2, pl.ds(at, 16), :] = here_rate
            fields[1 - of][pl.ds(edge + at, 16), :] = value
            keep(1 - of, at, value)

        sweep(of, update)
        listen(n, 1 - of)

    def forward_pair(k, _):
        forward(2 * k + 1, 0)
        forward(2 * k + 2, 1)
        return 0

    lax.fori_loop(0, (nstep - 1) // 2, forward_pair, 0)
    if nstep % 2 == 0:
        forward(nstep - 1, 0)

    step_lane = lax.broadcasted_iota(jnp.int32, (nrec, nstep), 1)

    def compare(n, total):
        picked = jnp.sum(rec_rows[n] * pick_ref[...], axis=1, keepdims=True)
        total = jnp.where(step_lane == n, picked, total)
        seen = jnp.sum(jnp.where(step_lane == n, obs_ref[...], 0.0), axis=1, keepdims=True)
        rec_rows[n] = jnp.dot(
            same_ref[...], pick_ref[...] * (picked - seen),
            preferred_element_type=jnp.float32, precision=lax.Precision.HIGHEST,
        )
        return total

    records = lax.fori_loop(0, nstep, compare, jnp.zeros((nrec, nstep), jnp.float32))
    mis_ref[...] = records - obs_ref[...]

    def inject(n):
        def take(r, _):
            moved[pl.ds(r, 1), :] = rate[pl.ds(rec_ref[r], 1), :]
            return 0

        lax.fori_loop(0, nrec, take, 0, unroll=16)
        moved[...] = moved[...] + rec_rows[n]

        def put(r, _):
            rate[pl.ds(rec_ref[r], 1), :] = moved[pl.ds(r, 1), :]
            return 0

        lax.fori_loop(0, nrec, put, 0, unroll=16)

    def clear(at):
        rate[pl.ds(at, 16), :] = jnp.zeros((16, LANES), jnp.float32)

    rows16(clear)
    inject(nstep - 1)

    def last(at):
        value = rate[pl.ds(at, 16), :]
        field_a[pl.ds(edge + at, 16), :] = value
        dense[pl.ds(at, 16), :] = hist[(nstep - 1) % 2][(nstep - 1) // 2, pl.ds(at, 16), :] * value
        keep(0, at, value)

    rows16(last)
    multiply(0, 0, taps_a)

    def backward(n, of):
        inject(n - 1)

        def update(at, here, lap):
            here_rate = rate[pl.ds(at, 16), :] + speed[pl.ds(at, 16), :] * lap
            value = here + here_rate
            rate[pl.ds(at, 16), :] = here_rate
            fields[1 - of][pl.ds(edge + at, 16), :] = value
            dense[pl.ds(at, 16), :] = dense[pl.ds(at, 16), :] + hist[(nstep + of) % 2][(n - 1) // 2, pl.ds(at, 16), :] * here_rate
            keep(1 - of, at, value)

        sweep(of, update)

    def backward_pair(k, _):
        backward(nstep - 1 - 2 * k, 0)
        backward(nstep - 2 - 2 * k, 1)
        return 0

    lax.fori_loop(0, (nstep - 2) // 2, backward_pair, 0)
    if nstep % 2 == 1:
        backward(2, 0)
    end = fields[nstep % 2]

    def finish(at):
        image = dense[pl.ds(at, 16), :] - hist_a[0, pl.ds(at, 16), :] * end[pl.ds(edge + at, 16), :]
        dense[pl.ds(at, 16), :] = (2.0 / region[pl.ds(at, 16), :]) * image

    rows16(finish)

    for r in range(held):
        @pl.when(give_ref[r] >= 0)
        def _():
            give(r).start()

    for r in range(held):
        blank(r).wait()


def shot(aper, targets, take, give, rec_at, wavelet, pieces, sources, picks, same, observed):
    shape = pieces[0].shape
    slab = shape[1] * shape[2]
    ny, nz = shape[2:]
    cells = aper * slab
    held = give.shape[0]
    nstep, nrec = wavelet.shape[0], rec_at.shape[0]
    in_y = band(ny, CENTER_Y)
    none = np.zeros_like(in_y)
    mat_y = np.block([[in_y, in_y, none, none], [none, none, in_y, in_y]])
    in_z = band(nz, CENTER_Z)
    mat_z = np.concatenate([in_z, in_z], axis=0)
    smem = pl.BlockSpec(memory_space=pltpu.SMEM)
    vmem = pl.BlockSpec(memory_space=pltpu.VMEM)
    hbm = pl.BlockSpec(memory_space=pl.ANY)
    f32 = jnp.float32
    edge = REACH * ny
    *grads, misfit = pl.pallas_call(
        functools.partial(kernel, len(pieces), targets),
        out_shape=(
            *[jax.ShapeDtypeStruct((held // targets, slab, nz), f32)] * targets,
            jax.ShapeDtypeStruct((nrec, nstep), f32),
        ),
        in_specs=[smem] * 4 + [hbm] + [vmem] * 5 + [hbm] * len(pieces),
        out_specs=(*[hbm] * targets, vmem),
        scratch_shapes=[
            pltpu.VMEM(((nstep + 1) // 2, cells, nz), f32),
            pltpu.VMEM((nstep // 2, cells, nz), f32),
            pltpu.VMEM((cells + 2 * edge, nz), f32),
            pltpu.VMEM((cells + 2 * edge, nz), f32),
            pltpu.VMEM((cells, 2 * nz), jnp.bfloat16),
            pltpu.VMEM((cells, 2 * nz), jnp.bfloat16),
            pltpu.VMEM((GROUP * ny, nz), f32),
            pltpu.VMEM((GROUP * ny, nz), f32),
            pltpu.VMEM((cells, nz), f32),
            pltpu.VMEM((cells, nz), f32),
            pltpu.VMEM((cells, nz), f32),
            pltpu.VMEM((cells, nz), f32),
            pltpu.VMEM((nstep, nrec, nz), f32),
            pltpu.VMEM((nrec, nz), f32),
            pltpu.SemaphoreType.DMA((aper,)),
            pltpu.SemaphoreType.DMA,
            pltpu.SemaphoreType.DMA((held,)),
        ],
        compiler_params=pltpu.CompilerParams(vmem_limit_bytes=60 * 1024 * 1024),
        name="shot_gradient",
    )(
        take, give, rec_at, wavelet, sources, picks, same, observed,
        jnp.asarray(mat_y, jnp.bfloat16), jnp.asarray(mat_z, jnp.bfloat16),
        *[piece.reshape(-1, slab, nz) for piece in pieces],
    )
    return grads, misfit


SIDE_Z, SIDE_Y, SIDE_CORE = 4, 2, 2
Z_ORDER = (0, 2, 1, 3)


def place(z, y, core):
    return (z * SIDE_Y + y) * SIDE_CORE + core


def trade(block, z=0, y=0, core=0):
    flip = place(z, y, core)
    return lax.ppermute(block, "shot", [(i, i ^ flip) for i in range(SIDE_Z * SIDE_Y * SIDE_CORE)])


def collect(velocity):
    first, second = velocity[:1], velocity[1:]
    beside = trade(second, y=1)
    first = jnp.concatenate([first, trade(first, z=2)])
    second = jnp.concatenate([second, beside])
    second = jnp.concatenate([second, trade(second, z=2)])
    first = jnp.concatenate([first, trade(first, z=1)])
    pieces = [first, second, trade(first, y=1), trade(second, z=1)]
    return pieces + [trade(piece, core=1) for piece in pieces]


def collected():
    offsets = []
    for core in range(SIDE_CORE):
        offsets += [(place(a, 0, core), 0) for a in Z_ORDER]
        offsets += [(place(a, b, core), 1) for a in Z_ORDER[:2] for b in range(SIDE_Y)]
        offsets += [(place(a, 1, core), 0) for a in Z_ORDER]
        offsets += [(place(a, b, core), 1) for a in Z_ORDER[2:] for b in range(SIDE_Y)]
    return offsets


def handed():
    offsets = []
    for core in range(SIDE_CORE):
        offsets += [(place(a, b, core), 0) for b in range(SIDE_Y) for a in Z_ORDER]
        offsets += [(place(a, b, core), 1) for a in Z_ORDER for b in range(SIDE_Y)]
    return offsets


def reduce(grads):
    first, second, far_first, far_second = grads
    first = first + trade(far_first, core=1)
    second = second + trade(far_second, core=1)
    first, second = first[:4] + trade(first[4:], y=1), second[:4] + trade(second[4:], z=1)
    first, second = first[:2] + trade(first[2:], z=1), second[:2] + trade(second[2:], z=2)
    first, second = first[:1] + trade(first[1:], z=2), second[:1] + trade(second[1:], y=1)
    return jnp.concatenate([first, second])


def shards(velocity, tile_owner, aperture, source_at, source_amp, receivers, wavelet, observed):
    devices = lax.axis_size("shot")
    me = lax.axis_index("shot")
    per_dev = velocity.shape[0]
    slabs = aperture[0]
    aper = slabs.shape[0]
    nz = velocity.shape[3]
    store_rows = tile_owner[slabs] * per_dev + slabs // devices
    split = devices == SIDE_Z * SIDE_Y * SIDE_CORE and per_dev == 2
    if split:
        pieces = collect(velocity)
        taken, given = collected(), handed()
        outs = 2 * SIDE_CORE
    else:
        pieces = [lax.all_gather(velocity, "shot", axis=0, tiled=True)]
        taken = given = [(d, r) for d in range(devices) for r in range(per_dev)]
        me = 0
        outs = 1

    def slots(offsets):
        at = np.asarray(offsets, np.int32)
        rows = (me ^ at[:, 0]) * per_dev + at[:, 1]
        hit = rows[:, None] == store_rows[None, :]
        return jnp.max(jnp.where(hit, jnp.arange(aper, dtype=jnp.int32)[None, :], -1), axis=1)

    cells = aper * velocity.shape[1] * velocity.shape[2]
    sources = jnp.zeros((cells * nz,), jnp.float32).at[source_at[0]].add(source_amp[0]).reshape(cells, nz)
    rec_at = receivers[0] // nz
    lane = receivers[0] % nz
    picks = (lane[:, None] == jnp.arange(nz, dtype=jnp.int32)[None, :]).astype(jnp.float32)
    same = (rec_at[:, None] == rec_at[None, :]).astype(jnp.float32)
    grads, misfit = shot(
        aper, outs, slots(taken), slots(given), rec_at, wavelet, pieces, sources, picks, same, observed[0].T
    )
    if split:
        gradient = reduce(grads)
    else:
        gradient = lax.psum_scatter(grads[0], "shot", scatter_dimension=0, tiled=True)
    return (gradient.reshape(velocity.shape), misfit.T[None])


def solution(mesh):
    in_specs = (
        P(("groups", "shot"), None, None, None),
        P(),
        P(("groups", "shot"), None),
        P(("groups", "shot"), None),
        P(("groups", "shot"), None),
        P(("groups", "shot"), None),
        P(),
        P(("groups", "shot"), None, None),
    )
    out_specs = (P(("groups", "shot"), None, None, None), P(("groups", "shot"), None, None))
    return jax.shard_map(shards, mesh=mesh, in_specs=in_specs, out_specs=out_specs, check_vma=False)
```

```python
import functools

import jax
import jax.numpy as jnp
import numpy as np
from jax import lax
from jax.experimental import pallas as pl
from jax.experimental.pallas import tpu as pltpu
from jax.sharding import PartitionSpec as P

STEP_RATIO = 0.1
TAPS = (63.0, -7.875, 1.0, -0.0703125)
CENTER_Z = -336.0
CENTER_Y = -0.328125
SCALE = 128.0 / 5040.0
REACH = 4
LANES = 128
GROUP = 8


def band(size, center):
    out = np.zeros((size, size), np.float32)
    np.fill_diagonal(out, center)
    for k, tap in enumerate(TAPS, 1):
        at = np.arange(size - k)
        out[at, at + k] = tap
        out[at + k, at] = tap
    return out


def kernel(
    sources, targets, take_ref, give_ref, rec_ref, wav_ref, src_hbm, pick_ref, same_ref, obs_ref, mat_y_ref, mat_z_ref,
    *refs,
):
    vel_refs, refs = refs[:sources], refs[sources:]
    grad_refs, refs = refs[:targets], refs[targets:]
    (
        mis_ref, hist_a, hist_b, field_a, field_b, halves_a, halves_b, taps_a, taps_b,
        speed, region, dense, rate, rec_rows, moved, in_sem, src_sem, out_sem,
    ) = refs
    nstep = wav_ref.shape[0]
    cells = speed.shape[0]
    nrec = pick_ref.shape[0]
    ny = mat_y_ref.shape[0] // 2
    per, slab = vel_refs[0].shape[:2]
    out_per = grad_refs[0].shape[0]
    aper = cells // slab
    edge = REACH * ny
    block = GROUP * ny
    groups = cells // block
    held = give_ref.shape[0]

    def fetch(i, j):
        at = pl.multiple_of(j * slab, slab)
        return pltpu.make_async_copy(
            vel_refs[i // per].at[i % per], region.at[pl.ds(at, slab), :], in_sem.at[j]
        )

    def blank(r):
        return pltpu.make_async_copy(
            field_a.at[pl.ds(0, slab), :], grad_refs[r // out_per].at[r % out_per], out_sem.at[r]
        )

    def give(r):
        at = pl.multiple_of(give_ref[r] * slab, slab)
        return pltpu.make_async_copy(
            dense.at[pl.ds(at, slab), :], grad_refs[r // out_per].at[r % out_per], out_sem.at[r]
        )

    source = pltpu.make_async_copy(src_hbm, dense, src_sem)
    source.start()
    for i in range(sources * per):
        @pl.when(take_ref[i] >= 0)
        def _():
            fetch(i, take_ref[i]).start()

    zeros = jnp.zeros((edge, LANES), jnp.float32)
    for field in (field_a, field_b):
        field[0:edge, :] = zeros
        field[edge + cells : edge + cells + edge, :] = zeros

    for r in range(held):
        @pl.when(give_ref[r] < 0)
        def _():
            blank(r).start()

    fields = (field_a, field_b)
    hist = (hist_a, hist_b)
    halves = (halves_a, halves_b)

    def keep(to, at, value):
        high = value.astype(jnp.bfloat16)
        halves[to][pl.ds(at, 16), 0:LANES] = high
        halves[to][pl.ds(at, 16), LANES : 2 * LANES] = (value - high.astype(jnp.float32)).astype(jnp.bfloat16)

    def listen(n, to):
        def body(r, _):
            rec_rows[n, pl.ds(r, 1), :] = fields[to][pl.ds(edge + rec_ref[r], 1), :]
            return 0

        lax.fori_loop(0, nrec, body, 0, unroll=64)

    def multiply(base, of, taps):
        both = halves[of][pl.ds(base, block), :]
        along_z = jnp.dot(both, mat_z_ref[...], preferred_element_type=jnp.float32)
        plane = [both[i * ny : (i + 1) * ny] for i in range(GROUP)]
        cols = []
        for i in range(0, GROUP, 2):
            cols.append(
                jnp.concatenate(
                    [plane[i][:, :LANES], plane[i][:, LANES:], plane[i + 1][:, :LANES], plane[i + 1][:, LANES:]],
                    axis=0,
                )
            )
        along_y = jnp.dot(mat_y_ref[...], jnp.concatenate(cols, axis=1), preferred_element_type=jnp.float32)
        for i in range(GROUP):
            taps[i * ny : (i + 1) * ny, :] = (
                along_z[i * ny : (i + 1) * ny]
                + along_y[(i % 2) * ny : (i % 2 + 1) * ny, (i // 2) * LANES : (i // 2 + 1) * LANES]
            )

    def combine(base, of, taps, update):
        for j in range(0, ny, 16):
            near = [fields[of][pl.ds(base + d * ny + j, 16), :] for d in range(GROUP + 2 * REACH)]
            for i in range(GROUP):
                lap = near[i + 4 - 3] + near[i + 4 + 3]
                lap = lap + TAPS[0] * (near[i + 4 - 1] + near[i + 4 + 1])
                lap = lap + TAPS[1] * (near[i + 4 - 2] + near[i + 4 + 2])
                lap = lap + TAPS[3] * (near[i + 4 - 4] + near[i + 4 + 4])
                lap = lap + taps[i * ny + j : i * ny + j + 16, :]
                at = base + i * ny + j
                update(at if isinstance(at, int) else pl.multiple_of(at, 16), near[i + 4], lap)

    def sweep(of, update):
        def body(g, _):
            base = pl.multiple_of(g * (2 * block), 2 * block)
            multiply(base + block, of, taps_b)
            combine(base, of, taps_a, update)
            multiply(base + 2 * block, of, taps_a)
            combine(base + block, of, taps_b, update)
            return 0

        lax.fori_loop(0, groups // 2 - 1, body, 0, unroll=True)
        base = (groups - 2) * block
        multiply(base + block, of, taps_b)
        combine(base, of, taps_a, update)
        multiply(0, 1 - of, taps_a)
        combine(base + block, of, taps_b, update)

    def rows16(fn):
        def body(g, _):
            fn(pl.multiple_of(g * 16, 16))
            return 0

        lax.fori_loop(0, cells // 16, body, 0, unroll=16)

    source.wait()

    def first(at):
        value = wav_ref[0] * dense[pl.ds(at, 16), :]
        hist_a[0, pl.ds(at, 16), :] = value
        field_a[pl.ds(edge + at, 16), :] = value
        keep(0, at, value)

    rows16(first)
    multiply(0, 0, taps_a)
    listen(0, 0)

    for j in range(aper):
        fetch(0, j).wait()

    def squared(at):
        scaled = STEP_RATIO * region[pl.ds(at, 16), :]
        speed[pl.ds(at, 16), :] = (scaled * scaled) * SCALE

    rows16(squared)

    def forward(n, of):
        strength = wav_ref[n]

        def update(at, here, lap):
            here_rate = hist[of][(n - 1) // 2, pl.ds(at, 16), :] + (
                speed[pl.ds(at, 16), :] * lap + strength * dense[pl.ds(at, 16), :]
            )
            value = here + here_rate
            hist[1 - of][n // 2, pl.ds(at, 16), :] = here_rate
            fields[1 - of][pl.ds(edge + at, 16), :] = value
            keep(1 - of, at, value)

        sweep(of, update)
        listen(n, 1 - of)

    def forward_pair(k, _):
        forward(2 * k + 1, 0)
        forward(2 * k + 2, 1)
        return 0

    lax.fori_loop(0, (nstep - 1) // 2, forward_pair, 0)
    if nstep % 2 == 0:
        forward(nstep - 1, 0)

    step_lane = lax.broadcasted_iota(jnp.int32, (nrec, nstep), 1)

    def compare(n, total):
        picked = jnp.sum(rec_rows[n] * pick_ref[...], axis=1, keepdims=True)
        total = jnp.where(step_lane == n, picked, total)
        seen = jnp.sum(jnp.where(step_lane == n, obs_ref[...], 0.0), axis=1, keepdims=True)
        rec_rows[n] = jnp.dot(
            same_ref[...], pick_ref[...] * (picked - seen),
            preferred_element_type=jnp.float32, precision=lax.Precision.HIGHEST,
        )
        return total

    records = jnp.zeros((nrec, nstep), jnp.float32)
    for n in range(nstep):
        records = compare(n, records)
    mis_ref[...] = records - obs_ref[...]

    def inject(n):
        def take(r, _):
            moved[pl.ds(r, 1), :] = rate[pl.ds(rec_ref[r], 1), :]
            return 0

        lax.fori_loop(0, nrec, take, 0, unroll=64)
        moved[...] = moved[...] + rec_rows[n]

        def put(r, _):
            rate[pl.ds(rec_ref[r], 1), :] = moved[pl.ds(r, 1), :]
            return 0

        lax.fori_loop(0, nrec, put, 0, unroll=64)

    def clear(at):
        rate[pl.ds(at, 16), :] = jnp.zeros((16, LANES), jnp.float32)

    rows16(clear)
    inject(nstep - 1)

    def last(at):
        value = rate[pl.ds(at, 16), :]
        field_a[pl.ds(edge + at, 16), :] = value
        dense[pl.ds(at, 16), :] = hist[(nstep - 1) % 2][(nstep - 1) // 2, pl.ds(at, 16), :] * value
        keep(0, at, value)

    rows16(last)
    multiply(0, 0, taps_a)

    def backward(n, of):
        inject(n - 1)

        def update(at, here, lap):
            here_rate = rate[pl.ds(at, 16), :] + speed[pl.ds(at, 16), :] * lap
            value = here + here_rate
            rate[pl.ds(at, 16), :] = here_rate
            fields[1 - of][pl.ds(edge + at, 16), :] = value
            dense[pl.ds(at, 16), :] = dense[pl.ds(at, 16), :] + hist[(nstep + of) % 2][(n - 1) // 2, pl.ds(at, 16), :] * here_rate
            keep(1 - of, at, value)

        sweep(of, update)

    def backward_pair(k, _):
        backward(nstep - 1 - 2 * k, 0)
        backward(nstep - 2 - 2 * k, 1)
        return 0

    lax.fori_loop(0, (nstep - 2) // 2, backward_pair, 0)
    if nstep % 2 == 1:
        backward(2, 0)
    end = fields[nstep % 2]

    def finish(at):
        image = dense[pl.ds(at, 16), :] - hist_a[0, pl.ds(at, 16), :] * end[pl.ds(edge + at, 16), :]
        dense[pl.ds(at, 16), :] = (2.0 / region[pl.ds(at, 16), :]) * image

    rows16(finish)

    for r in range(held):
        @pl.when(give_ref[r] >= 0)
        def _():
            give(r).start()

    for r in range(held):
        blank(r).wait()


def shot(aper, targets, take, give, rec_at, wavelet, pieces, sources, picks, same, observed):
    shape = pieces[0].shape
    slab = shape[1] * shape[2]
    ny, nz = shape[2:]
    cells = aper * slab
    held = give.shape[0]
    nstep, nrec = wavelet.shape[0], rec_at.shape[0]
    in_y = band(ny, CENTER_Y)
    none = np.zeros_like(in_y)
    mat_y = np.block([[in_y, in_y, none, none], [none, none, in_y, in_y]])
    in_z = band(nz, CENTER_Z)
    mat_z = np.concatenate([in_z, in_z], axis=0)
    smem = pl.BlockSpec(memory_space=pltpu.SMEM)
    vmem = pl.BlockSpec(memory_space=pltpu.VMEM)
    hbm = pl.BlockSpec(memory_space=pl.ANY)
    f32 = jnp.float32
    edge = REACH * ny
    *grads, misfit = pl.pallas_call(
        functools.partial(kernel, len(pieces), targets),
        out_shape=(
            *[jax.ShapeDtypeStruct((held // targets, slab, nz), f32)] * targets,
            jax.ShapeDtypeStruct((nrec, nstep), f32),
        ),
        in_specs=[smem] * 4 + [hbm] + [vmem] * 5 + [hbm] * len(pieces),
        out_specs=(*[hbm] * targets, vmem),
        scratch_shapes=[
            pltpu.VMEM(((nstep + 1) // 2, cells, nz), f32),
            pltpu.VMEM((nstep // 2, cells, nz), f32),
            pltpu.VMEM((cells + 2 * edge, nz), f32),
            pltpu.VMEM((cells + 2 * edge, nz), f32),
            pltpu.VMEM((cells, 2 * nz), jnp.bfloat16),
            pltpu.VMEM((cells, 2 * nz), jnp.bfloat16),
            pltpu.VMEM((GROUP * ny, nz), f32),
            pltpu.VMEM((GROUP * ny, nz), f32),
            pltpu.VMEM((cells, nz), f32),
            pltpu.VMEM((cells, nz), f32),
            pltpu.VMEM((cells, nz), f32),
            pltpu.VMEM((cells, nz), f32),
            pltpu.VMEM((nstep, nrec, nz), f32),
            pltpu.VMEM((nrec, nz), f32),
            pltpu.SemaphoreType.DMA((aper,)),
            pltpu.SemaphoreType.DMA,
            pltpu.SemaphoreType.DMA((held,)),
        ],
        compiler_params=pltpu.CompilerParams(vmem_limit_bytes=60 * 1024 * 1024),
        name="shot_gradient",
    )(
        take, give, rec_at, wavelet, sources, picks, same, observed,
        jnp.asarray(mat_y, jnp.bfloat16), jnp.asarray(mat_z, jnp.bfloat16),
        *[piece.reshape(-1, slab, nz) for piece in pieces],
    )
    return grads, misfit


SIDE_Z, SIDE_Y, SIDE_CORE = 4, 2, 2
Z_ORDER = (0, 2, 1, 3)


def place(z, y, core):
    return (z * SIDE_Y + y) * SIDE_CORE + core


def trade(block, z=0, y=0, core=0):
    flip = place(z, y, core)
    return lax.ppermute(block, "shot", [(i, i ^ flip) for i in range(SIDE_Z * SIDE_Y * SIDE_CORE)])


def collect(velocity):
    first, second = velocity[:1], velocity[1:]
    beside = trade(second, y=1)
    first = jnp.concatenate([first, trade(first, z=2)])
    second = jnp.concatenate([second, beside])
    second = jnp.concatenate([second, trade(second, z=2)])
    first = jnp.concatenate([first, trade(first, z=1)])
    pieces = [first, second, trade(first, y=1), trade(second, z=1)]
    return pieces + [trade(piece, core=1) for piece in pieces]


def collected():
    offsets = []
    for core in range(SIDE_CORE):
        offsets += [(place(a, 0, core), 0) for a in Z_ORDER]
        offsets += [(place(a, b, core), 1) for a in Z_ORDER[:2] for b in range(SIDE_Y)]
        offsets += [(place(a, 1, core), 0) for a in Z_ORDER]
        offsets += [(place(a, b, core), 1) for a in Z_ORDER[2:] for b in range(SIDE_Y)]
    return offsets


def handed():
    offsets = []
    for core in range(SIDE_CORE):
        offsets += [(place(a, b, core), 0) for b in range(SIDE_Y) for a in Z_ORDER]
        offsets += [(place(a, b, core), 1) for a in Z_ORDER for b in range(SIDE_Y)]
    return offsets


def reduce(grads):
    first, second, far_first, far_second = grads
    first = first + trade(far_first, core=1)
    second = second + trade(far_second, core=1)
    first, second = first[:4] + trade(first[4:], y=1), second[:4] + trade(second[4:], z=1)
    first, second = first[:2] + trade(first[2:], z=1), second[:2] + trade(second[2:], z=2)
    first, second = first[:1] + trade(first[1:], z=2), second[:1] + trade(second[1:], y=1)
    return jnp.concatenate([first, second])


def shards(velocity, tile_owner, aperture, source_at, source_amp, receivers, wavelet, observed):
    devices = lax.axis_size("shot")
    me = lax.axis_index("shot")
    per_dev = velocity.shape[0]
    slabs = aperture[0]
    aper = slabs.shape[0]
    nz = velocity.shape[3]
    store_rows = tile_owner[slabs] * per_dev + slabs // devices
    split = devices == SIDE_Z * SIDE_Y * SIDE_CORE and per_dev == 2
    if split:
        pieces = collect(velocity)
        taken, given = collected(), handed()
        outs = 2 * SIDE_CORE
    else:
        pieces = [lax.all_gather(velocity, "shot", axis=0, tiled=True)]
        taken = given = [(d, r) for d in range(devices) for r in range(per_dev)]
        me = 0
        outs = 1

    def slots(offsets):
        at = np.asarray(offsets, np.int32)
        rows = (me ^ at[:, 0]) * per_dev + at[:, 1]
        hit = rows[:, None] == store_rows[None, :]
        return jnp.max(jnp.where(hit, jnp.arange(aper, dtype=jnp.int32)[None, :], -1), axis=1)

    cells = aper * velocity.shape[1] * velocity.shape[2]
    sources = jnp.zeros((cells * nz,), jnp.float32).at[source_at[0]].add(source_amp[0]).reshape(cells, nz)
    rec_at = receivers[0] // nz
    lane = receivers[0] % nz
    picks = (lane[:, None] == jnp.arange(nz, dtype=jnp.int32)[None, :]).astype(jnp.float32)
    same = (rec_at[:, None] == rec_at[None, :]).astype(jnp.float32)
    grads, misfit = shot(
        aper, outs, slots(taken), slots(given), rec_at, wavelet, pieces, sources, picks, same, observed[0].T
    )
    if split:
        gradient = reduce(grads)
    else:
        gradient = lax.psum_scatter(grads[0], "shot", scatter_dimension=0, tiled=True)
    return (gradient.reshape(velocity.shape), misfit.T[None])


def solution(mesh):
    in_specs = (
        P(("groups", "shot"), None, None, None),
        P(),
        P(("groups", "shot"), None),
        P(("groups", "shot"), None),
        P(("groups", "shot"), None),
        P(("groups", "shot"), None),
        P(),
        P(("groups", "shot"), None, None),
    )
    out_specs = (P(("groups", "shot"), None, None, None), P(("groups", "shot"), None, None))
    return jax.shard_map(shards, mesh=mesh, in_specs=in_specs, out_specs=out_specs, check_vma=False)
```

```python
import functools

import jax
import jax.numpy as jnp
import numpy as np
from jax import lax
from jax.experimental import pallas as pl
from jax.experimental.pallas import tpu as pltpu
from jax.sharding import PartitionSpec as P

STEP_RATIO = 0.1
TAPS = (63.0, -7.875, 1.0, -0.0703125)
CENTER_Z = -336.0
CENTER_Y = -0.328125
SCALE = 128.0 / 5040.0
REACH = 4
LANES = 128
GROUP = 16


def band(size, center):
    out = np.zeros((size, size), np.float32)
    np.fill_diagonal(out, center)
    for k, tap in enumerate(TAPS, 1):
        at = np.arange(size - k)
        out[at, at + k] = tap
        out[at + k, at] = tap
    return out


def kernel(
    sources, targets, take_ref, give_ref, rec_ref, wav_ref, src_hbm, pick_ref, same_ref, obs_ref, mat_y_ref, mat_z_ref,
    *refs,
):
    vel_refs, refs = refs[:sources], refs[sources:]
    grad_refs, refs = refs[:targets], refs[targets:]
    (
        mis_ref, hist_a, hist_b, field_a, field_b, halves_a, halves_b, taps_a, taps_b,
        speed, region, dense, rate, rec_rows, moved, in_sem, src_sem, out_sem,
    ) = refs
    nstep = wav_ref.shape[0]
    cells = speed.shape[0]
    nrec = pick_ref.shape[0]
    ny = mat_y_ref.shape[0] // 2
    per, slab = vel_refs[0].shape[:2]
    out_per = grad_refs[0].shape[0]
    aper = cells // slab
    edge = REACH * ny
    block = GROUP * ny
    groups = cells // block
    held = give_ref.shape[0]

    def fetch(i, j):
        at = pl.multiple_of(j * slab, slab)
        return pltpu.make_async_copy(
            vel_refs[i // per].at[i % per], region.at[pl.ds(at, slab), :], in_sem.at[j]
        )

    def blank(r):
        return pltpu.make_async_copy(
            field_a.at[pl.ds(0, slab), :], grad_refs[r // out_per].at[r % out_per], out_sem.at[r]
        )

    def give(r):
        at = pl.multiple_of(give_ref[r] * slab, slab)
        return pltpu.make_async_copy(
            dense.at[pl.ds(at, slab), :], grad_refs[r // out_per].at[r % out_per], out_sem.at[r]
        )

    source = pltpu.make_async_copy(src_hbm, dense, src_sem)
    source.start()
    for i in range(sources * per):
        @pl.when(take_ref[i] >= 0)
        def _():
            fetch(i, take_ref[i]).start()

    zeros = jnp.zeros((edge, LANES), jnp.float32)
    for field in (field_a, field_b):
        field[0:edge, :] = zeros
        field[edge + cells : edge + cells + edge, :] = zeros

    for r in range(held):
        @pl.when(give_ref[r] < 0)
        def _():
            blank(r).start()

    fields = (field_a, field_b)
    hist = (hist_a, hist_b)
    halves = (halves_a, halves_b)

    def keep(to, at, value):
        high = value.astype(jnp.bfloat16)
        halves[to][pl.ds(at, 16), 0:LANES] = high
        halves[to][pl.ds(at, 16), LANES : 2 * LANES] = (value - high.astype(jnp.float32)).astype(jnp.bfloat16)

    def listen(n, to):
        def body(r, _):
            rec_rows[n, pl.ds(r, 1), :] = fields[to][pl.ds(edge + rec_ref[r], 1), :]
            return 0

        lax.fori_loop(0, nrec, body, 0, unroll=64)

    def multiply(base, of, taps):
        both = halves[of][pl.ds(base, block), :]
        along_z = jnp.dot(both, mat_z_ref[...], preferred_element_type=jnp.float32)
        plane = [both[i * ny : (i + 1) * ny] for i in range(GROUP)]
        cols = []
        for i in range(0, GROUP, 2):
            cols.append(
                jnp.concatenate(
                    [plane[i][:, :LANES], plane[i][:, LANES:], plane[i + 1][:, :LANES], plane[i + 1][:, LANES:]],
                    axis=0,
                )
            )
        along_y = jnp.dot(mat_y_ref[...], jnp.concatenate(cols, axis=1), preferred_element_type=jnp.float32)
        for i in range(GROUP):
            taps[i * ny : (i + 1) * ny, :] = (
                along_z[i * ny : (i + 1) * ny]
                + along_y[(i % 2) * ny : (i % 2 + 1) * ny, (i // 2) * LANES : (i // 2 + 1) * LANES]
            )

    def combine(base, of, taps, update):
        for j in range(0, ny, 16):
            for h in range(0, GROUP, 4):
                near = [fields[of][pl.ds(base + (h + d) * ny + j, 16), :] for d in range(4 + 2 * REACH)]
                for i in range(4):
                    lap = near[i + 4 - 3] + near[i + 4 + 3]
                    lap = lap + TAPS[0] * (near[i + 4 - 1] + near[i + 4 + 1])
                    lap = lap + TAPS[1] * (near[i + 4 - 2] + near[i + 4 + 2])
                    lap = lap + TAPS[3] * (near[i + 4 - 4] + near[i + 4 + 4])
                    at = (h + i) * ny + j
                    lap = lap + taps[at : at + 16, :]
                    at = base + at
                    update(at if isinstance(at, int) else pl.multiple_of(at, 16), near[i + 4], lap)

    def sweep(of, update, ahead=True):
        def body(g, _):
            base = pl.multiple_of(g * (2 * block), 2 * block)
            multiply(base + block, of, taps_b)
            combine(base, of, taps_a, update)
            multiply(base + 2 * block, of, taps_a)
            combine(base + block, of, taps_b, update)
            return 0

        lax.fori_loop(0, groups // 2 - 1, body, 0, unroll=True)
        base = (groups - 2) * block
        multiply(base + block, of, taps_b)
        combine(base, of, taps_a, update)
        if ahead:
            multiply(0, 1 - of, taps_a)
        combine(base + block, of, taps_b, update)

    def rows16(fn):
        def body(g, _):
            fn(pl.multiple_of(g * 16, 16))
            return 0

        lax.fori_loop(0, cells // 16, body, 0, unroll=16)

    source.wait()

    def first(at):
        value = wav_ref[0] * dense[pl.ds(at, 16), :]
        hist_a[0, pl.ds(at, 16), :] = value
        field_a[pl.ds(edge + at, 16), :] = value
        keep(0, at, value)

    rows16(first)
    multiply(0, 0, taps_a)
    listen(0, 0)

    for j in range(aper):
        fetch(0, j).wait()

    def squared(at):
        scaled = STEP_RATIO * region[pl.ds(at, 16), :]
        speed[pl.ds(at, 16), :] = (scaled * scaled) * SCALE

    rows16(squared)

    def forward(n, of, ahead=True):
        strength = wav_ref[n]

        def update(at, here, lap):
            here_rate = hist[of][(n - 1) // 2, pl.ds(at, 16), :] + (
                speed[pl.ds(at, 16), :] * lap + strength * dense[pl.ds(at, 16), :]
            )
            value = here + here_rate
            hist[1 - of][n // 2, pl.ds(at, 16), :] = here_rate
            fields[1 - of][pl.ds(edge + at, 16), :] = value
            if ahead:
                keep(1 - of, at, value)

        sweep(of, update, ahead)
        listen(n, 1 - of)

    def forward_pair(k, _):
        forward(2 * k + 1, 0)
        forward(2 * k + 2, 1)
        return 0

    lax.fori_loop(0, (nstep - 1) // 2, forward_pair, 0)
    if nstep % 2 == 0:
        forward(nstep - 1, 0, False)

    step_lane = lax.broadcasted_iota(jnp.int32, (nrec, nstep), 1)

    def compare(n, total):
        picked = jnp.sum(rec_rows[n] * pick_ref[...], axis=1, keepdims=True)
        total = jnp.where(step_lane == n, picked, total)
        seen = jnp.sum(jnp.where(step_lane == n, obs_ref[...], 0.0), axis=1, keepdims=True)
        rec_rows[n] = jnp.dot(
            same_ref[...], pick_ref[...] * (picked - seen),
            preferred_element_type=jnp.float32, precision=lax.Precision.HIGHEST,
        )
        return total

    records = jnp.zeros((nrec, nstep), jnp.float32)
    for n in range(nstep):
        records = compare(n, records)
    mis_ref[...] = records - obs_ref[...]

    def inject(n):
        def take(r, _):
            moved[pl.ds(r, 1), :] = rate[pl.ds(rec_ref[r], 1), :]
            return 0

        lax.fori_loop(0, nrec, take, 0, unroll=64)
        moved[...] = moved[...] + rec_rows[n]

        def put(r, _):
            rate[pl.ds(rec_ref[r], 1), :] = moved[pl.ds(r, 1), :]
            return 0

        lax.fori_loop(0, nrec, put, 0, unroll=64)

    def clear(at):
        rate[pl.ds(at, 16), :] = jnp.zeros((16, LANES), jnp.float32)

    rows16(clear)
    inject(nstep - 1)

    def last(at):
        value = rate[pl.ds(at, 16), :]
        field_a[pl.ds(edge + at, 16), :] = value
        dense[pl.ds(at, 16), :] = hist[(nstep - 1) % 2][(nstep - 1) // 2, pl.ds(at, 16), :] * value
        keep(0, at, value)

    rows16(last)
    multiply(0, 0, taps_a)

    def backward(n, of):
        inject(n - 1)

        def update(at, here, lap):
            here_rate = rate[pl.ds(at, 16), :] + speed[pl.ds(at, 16), :] * lap
            value = here + here_rate
            rate[pl.ds(at, 16), :] = here_rate
            fields[1 - of][pl.ds(edge + at, 16), :] = value
            dense[pl.ds(at, 16), :] = dense[pl.ds(at, 16), :] + hist[(nstep + of) % 2][(n - 1) // 2, pl.ds(at, 16), :] * here_rate
            keep(1 - of, at, value)

        sweep(of, update)

    def backward_pair(k, _):
        backward(nstep - 1 - 2 * k, 0)
        backward(nstep - 2 - 2 * k, 1)
        return 0

    lax.fori_loop(0, (nstep - 2) // 2, backward_pair, 0)
    if nstep % 2 == 1:
        backward(2, 0)
    end = fields[nstep % 2]

    def finish(at):
        image = dense[pl.ds(at, 16), :] - hist_a[0, pl.ds(at, 16), :] * end[pl.ds(edge + at, 16), :]
        dense[pl.ds(at, 16), :] = (2.0 / region[pl.ds(at, 16), :]) * image

    for r in range(held):
        @pl.when(give_ref[r] >= 0)
        def _():
            for j in range(0, slab, 16):
                finish(pl.multiple_of(give_ref[r] * slab + j, 16))
            give(r).start()

    for r in range(held):
        blank(r).wait()


def shot(aper, targets, take, give, rec_at, wavelet, pieces, sources, picks, same, observed):
    shape = pieces[0].shape
    slab = shape[1] * shape[2]
    ny, nz = shape[2:]
    cells = aper * slab
    held = give.shape[0]
    nstep, nrec = wavelet.shape[0], rec_at.shape[0]
    in_y = band(ny, CENTER_Y)
    none = np.zeros_like(in_y)
    mat_y = np.block([[in_y, in_y, none, none], [none, none, in_y, in_y]])
    in_z = band(nz, CENTER_Z)
    mat_z = np.concatenate([in_z, in_z], axis=0)
    smem = pl.BlockSpec(memory_space=pltpu.SMEM)
    vmem = pl.BlockSpec(memory_space=pltpu.VMEM)
    hbm = pl.BlockSpec(memory_space=pl.ANY)
    f32 = jnp.float32
    edge = REACH * ny
    *grads, misfit = pl.pallas_call(
        functools.partial(kernel, len(pieces), targets),
        out_shape=(
            *[jax.ShapeDtypeStruct((held // targets, slab, nz), f32)] * targets,
            jax.ShapeDtypeStruct((nrec, nstep), f32),
        ),
        in_specs=[smem] * 4 + [hbm] + [vmem] * 5 + [hbm] * len(pieces),
        out_specs=(*[hbm] * targets, vmem),
        scratch_shapes=[
            pltpu.VMEM(((nstep + 1) // 2, cells, nz), f32),
            pltpu.VMEM((nstep // 2, cells, nz), f32),
            pltpu.VMEM((cells + 2 * edge, nz), f32),
            pltpu.VMEM((cells + 2 * edge, nz), f32),
            pltpu.VMEM((cells, 2 * nz), jnp.bfloat16),
            pltpu.VMEM((cells, 2 * nz), jnp.bfloat16),
            pltpu.VMEM((GROUP * ny, nz), f32),
            pltpu.VMEM((GROUP * ny, nz), f32),
            pltpu.VMEM((cells, nz), f32),
            pltpu.VMEM((cells, nz), f32),
            pltpu.VMEM((cells, nz), f32),
            pltpu.VMEM((cells, nz), f32),
            pltpu.VMEM((nstep, nrec, nz), f32),
            pltpu.VMEM((nrec, nz), f32),
            pltpu.SemaphoreType.DMA((aper,)),
            pltpu.SemaphoreType.DMA,
            pltpu.SemaphoreType.DMA((held,)),
        ],
        compiler_params=pltpu.CompilerParams(vmem_limit_bytes=60 * 1024 * 1024),
        name="shot_gradient",
    )(
        take, give, rec_at, wavelet, sources, picks, same, observed,
        jnp.asarray(mat_y, jnp.bfloat16), jnp.asarray(mat_z, jnp.bfloat16),
        *[piece.reshape(-1, slab, nz) for piece in pieces],
    )
    return grads, misfit


SIDE_Z, SIDE_Y, SIDE_CORE = 4, 2, 2
Z_ORDER = (0, 2, 1, 3)


def place(z, y, core):
    return (z * SIDE_Y + y) * SIDE_CORE + core


def trade(block, z=0, y=0, core=0):
    flip = place(z, y, core)
    return lax.ppermute(block, "shot", [(i, i ^ flip) for i in range(SIDE_Z * SIDE_Y * SIDE_CORE)])


def collect(velocity):
    first, second = velocity[:1], velocity[1:]
    beside = trade(second, y=1)
    first = jnp.concatenate([first, trade(first, z=2)])
    second = jnp.concatenate([second, beside])
    second = jnp.concatenate([second, trade(second, z=2)])
    first = jnp.concatenate([first, trade(first, z=1)])
    pieces = [first, second, trade(first, y=1), trade(second, z=1)]
    return pieces + [trade(piece, core=1) for piece in pieces]


def collected():
    offsets = []
    for core in range(SIDE_CORE):
        offsets += [(place(a, 0, core), 0) for a in Z_ORDER]
        offsets += [(place(a, b, core), 1) for a in Z_ORDER[:2] for b in range(SIDE_Y)]
        offsets += [(place(a, 1, core), 0) for a in Z_ORDER]
        offsets += [(place(a, b, core), 1) for a in Z_ORDER[2:] for b in range(SIDE_Y)]
    return offsets


def handed():
    offsets = []
    for core in range(SIDE_CORE):
        offsets += [(place(a, b, core), 0) for b in range(SIDE_Y) for a in Z_ORDER]
        offsets += [(place(a, b, core), 1) for a in Z_ORDER for b in range(SIDE_Y)]
    return offsets


def reduce(grads):
    first, second, far_first, far_second = grads
    first = first + trade(far_first, core=1)
    second = second + trade(far_second, core=1)
    first, second = first[:4] + trade(first[4:], y=1), second[:4] + trade(second[4:], z=1)
    first, second = first[:2] + trade(first[2:], z=1), second[:2] + trade(second[2:], z=2)
    first, second = first[:1] + trade(first[1:], z=2), second[:1] + trade(second[1:], y=1)
    return jnp.concatenate([first, second])


def shards(velocity, tile_owner, aperture, source_at, source_amp, receivers, wavelet, observed):
    devices = lax.axis_size("shot")
    me = lax.axis_index("shot")
    per_dev = velocity.shape[0]
    slabs = aperture[0]
    aper = slabs.shape[0]
    nz = velocity.shape[3]
    store_rows = tile_owner[slabs] * per_dev + slabs // devices
    split = devices == SIDE_Z * SIDE_Y * SIDE_CORE and per_dev == 2
    if split:
        pieces = collect(velocity)
        taken, given = collected(), handed()
        outs = 2 * SIDE_CORE
    else:
        pieces = [lax.all_gather(velocity, "shot", axis=0, tiled=True)]
        taken = given = [(d, r) for d in range(devices) for r in range(per_dev)]
        me = 0
        outs = 1

    def slots(offsets):
        at = np.asarray(offsets, np.int32)
        rows = (me ^ at[:, 0]) * per_dev + at[:, 1]
        hit = rows[:, None] == store_rows[None, :]
        return jnp.max(jnp.where(hit, jnp.arange(aper, dtype=jnp.int32)[None, :], -1), axis=1)

    cells = aper * velocity.shape[1] * velocity.shape[2]
    sources = jnp.zeros((cells * nz,), jnp.float32).at[source_at[0]].add(source_amp[0]).reshape(cells, nz)
    rec_at = receivers[0] // nz
    lane = receivers[0] % nz
    picks = (lane[:, None] == jnp.arange(nz, dtype=jnp.int32)[None, :]).astype(jnp.float32)
    same = (rec_at[:, None] == rec_at[None, :]).astype(jnp.float32)
    grads, misfit = shot(
        aper, outs, slots(taken), slots(given), rec_at, wavelet, pieces, sources, picks, same, observed[0].T
    )
    if split:
        gradient = reduce(grads)
    else:
        gradient = lax.psum_scatter(grads[0], "shot", scatter_dimension=0, tiled=True)
    return (gradient.reshape(velocity.shape), misfit.T[None])


def solution(mesh):
    in_specs = (
        P(("groups", "shot"), None, None, None),
        P(),
        P(("groups", "shot"), None),
        P(("groups", "shot"), None),
        P(("groups", "shot"), None),
        P(("groups", "shot"), None),
        P(),
        P(("groups", "shot"), None, None),
    )
    out_specs = (P(("groups", "shot"), None, None, None), P(("groups", "shot"), None, None))
    return jax.shard_map(shards, mesh=mesh, in_specs=in_specs, out_specs=out_specs, check_vma=False)
```

```python
import functools

import jax
import jax.numpy as jnp
import numpy as np
from jax import lax
from jax.experimental import pallas as pl
from jax.experimental.pallas import tpu as pltpu
from jax.sharding import PartitionSpec as P

STEP_RATIO = 0.1
TAPS = (63.0, -7.875, 1.0, -0.0703125)
CENTER_Z = -336.0
CENTER_Y = -0.328125
SCALE = 128.0 / 5040.0
REACH = 4
LANES = 128
GROUP = 16


def band(size, center):
    out = np.zeros((size, size), np.float32)
    np.fill_diagonal(out, center)
    for k, tap in enumerate(TAPS, 1):
        at = np.arange(size - k)
        out[at, at + k] = tap
        out[at + k, at] = tap
    return out


def kernel(
    sources, targets, take_ref, give_ref, rec_ref, wav_ref, src_hbm, pick_ref, same_ref, obs_ref, mat_y_ref, mat_z_ref,
    *refs,
):
    vel_refs, refs = refs[:sources], refs[sources:]
    grad_refs, refs = refs[:targets], refs[targets:]
    (
        mis_ref, hist_a, hist_b, field_a, field_b, halves_a, halves_b, taps_a, taps_b,
        speed, region, dense, rate, rec_rows, moved, in_sem, src_sem, out_sem,
    ) = refs
    nstep = wav_ref.shape[0]
    cells = speed.shape[0]
    nrec = pick_ref.shape[0]
    ny = mat_y_ref.shape[0] // 2
    per, slab = vel_refs[0].shape[:2]
    out_per = grad_refs[0].shape[0]
    aper = cells // slab
    edge = REACH * ny
    block = GROUP * ny
    groups = cells // block
    held = give_ref.shape[0]

    def fetch(i, j):
        at = pl.multiple_of(j * slab, slab)
        return pltpu.make_async_copy(
            vel_refs[i // per].at[i % per], region.at[pl.ds(at, slab), :], in_sem.at[j]
        )

    def blank(r):
        return pltpu.make_async_copy(
            field_a.at[pl.ds(0, slab), :], grad_refs[r // out_per].at[r % out_per], out_sem.at[r]
        )

    def give(r):
        at = pl.multiple_of(give_ref[r] * slab, slab)
        return pltpu.make_async_copy(
            dense.at[pl.ds(at, slab), :], grad_refs[r // out_per].at[r % out_per], out_sem.at[r]
        )

    source = pltpu.make_async_copy(src_hbm, dense, src_sem)
    source.start()
    for i in range(sources * per):
        @pl.when(take_ref[i] >= 0)
        def _():
            fetch(i, take_ref[i]).start()

    zeros = jnp.zeros((edge, LANES), jnp.float32)
    for field in (field_a, field_b):
        field[0:edge, :] = zeros
        field[edge + cells : edge + cells + edge, :] = zeros

    for r in range(held):
        @pl.when(give_ref[r] < 0)
        def _():
            blank(r).start()

    fields = (field_a, field_b)
    hist = (hist_a, hist_b)
    halves = (halves_a, halves_b)

    def keep(to, at, value):
        high = value.astype(jnp.bfloat16)
        halves[to][pl.ds(at, 16), 0:LANES] = high
        halves[to][pl.ds(at, 16), LANES : 2 * LANES] = (value - high.astype(jnp.float32)).astype(jnp.bfloat16)

    def listen(n, to):
        def body(r, _):
            rec_rows[n, pl.ds(r, 1), :] = fields[to][pl.ds(edge + rec_ref[r], 1), :]
            return 0

        lax.fori_loop(0, nrec, body, 0, unroll=True)

    def multiply(base, of, taps):
        both = halves[of][pl.ds(base, block), :]
        along_z = jnp.dot(both, mat_z_ref[...], preferred_element_type=jnp.float32)
        plane = [both[i * ny : (i + 1) * ny] for i in range(GROUP)]
        cols = []
        for i in range(0, GROUP, 2):
            cols.append(
                jnp.concatenate(
                    [plane[i][:, :LANES], plane[i][:, LANES:], plane[i + 1][:, :LANES], plane[i + 1][:, LANES:]],
                    axis=0,
                )
            )
        along_y = jnp.dot(mat_y_ref[...], jnp.concatenate(cols, axis=1), preferred_element_type=jnp.float32)
        for i in range(GROUP):
            taps[i * ny : (i + 1) * ny, :] = (
                along_z[i * ny : (i + 1) * ny]
                + along_y[(i % 2) * ny : (i % 2 + 1) * ny, (i // 2) * LANES : (i // 2 + 1) * LANES]
            )

    def combine(base, of, taps, update):
        for j in range(0, ny, 16):
            for h in range(0, GROUP, 4):
                near = [fields[of][pl.ds(base + (h + d) * ny + j, 16), :] for d in range(4 + 2 * REACH)]
                for i in range(4):
                    lap = near[i + 4 - 3] + near[i + 4 + 3]
                    lap = lap + TAPS[0] * (near[i + 4 - 1] + near[i + 4 + 1])
                    lap = lap + TAPS[1] * (near[i + 4 - 2] + near[i + 4 + 2])
                    lap = lap + TAPS[3] * (near[i + 4 - 4] + near[i + 4 + 4])
                    at = (h + i) * ny + j
                    lap = lap + taps[at : at + 16, :]
                    at = base + at
                    update(at if isinstance(at, int) else pl.multiple_of(at, 16), near[i + 4], lap)

    def sweep(of, update, ahead=True):
        def body(g, _):
            base = pl.multiple_of(g * (2 * block), 2 * block)
            multiply(base + block, of, taps_b)
            combine(base, of, taps_a, update)
            multiply(base + 2 * block, of, taps_a)
            combine(base + block, of, taps_b, update)
            return 0

        lax.fori_loop(0, groups // 2 - 1, body, 0, unroll=True)
        base = (groups - 2) * block
        multiply(base + block, of, taps_b)
        combine(base, of, taps_a, update)
        if ahead:
            multiply(0, 1 - of, taps_a)
        combine(base + block, of, taps_b, update)

    def rows16(fn):
        def body(g, _):
            fn(pl.multiple_of(g * 16, 16))
            return 0

        lax.fori_loop(0, cells // 16, body, 0, unroll=16)

    source.wait()

    def first(at):
        value = wav_ref[0] * dense[pl.ds(at, 16), :]
        hist_a[0, pl.ds(at, 16), :] = value
        field_a[pl.ds(edge + at, 16), :] = value
        keep(0, at, value)

    rows16(first)
    multiply(0, 0, taps_a)
    listen(0, 0)

    for j in range(aper):
        fetch(0, j).wait()

    def squared(at):
        scaled = STEP_RATIO * region[pl.ds(at, 16), :]
        speed[pl.ds(at, 16), :] = (scaled * scaled) * SCALE

    rows16(squared)

    def forward(n, of, ahead=True):
        strength = wav_ref[n]

        def update(at, here, lap):
            here_rate = hist[of][(n - 1) // 2, pl.ds(at, 16), :] + (
                speed[pl.ds(at, 16), :] * lap + strength * dense[pl.ds(at, 16), :]
            )
            value = here + here_rate
            hist[1 - of][n // 2, pl.ds(at, 16), :] = here_rate
            fields[1 - of][pl.ds(edge + at, 16), :] = value
            if ahead:
                keep(1 - of, at, value)

        sweep(of, update, ahead)
        listen(n, 1 - of)

    def forward_pair(k, _):
        forward(2 * k + 1, 0)
        forward(2 * k + 2, 1)
        return 0

    lax.fori_loop(0, (nstep - 1) // 2, forward_pair, 0)
    if nstep % 2 == 0:
        forward(nstep - 1, 0, False)

    step_lane = lax.broadcasted_iota(jnp.int32, (nrec, nstep), 1)

    def compare(n, total):
        picked = jnp.sum(rec_rows[n] * pick_ref[...], axis=1, keepdims=True)
        total = jnp.where(step_lane == n, picked, total)
        seen = jnp.sum(jnp.where(step_lane == n, obs_ref[...], 0.0), axis=1, keepdims=True)
        rec_rows[n] = jnp.dot(
            same_ref[...], pick_ref[...] * (picked - seen),
            preferred_element_type=jnp.float32, precision=lax.Precision.HIGHEST,
        )
        return total

    records = jnp.zeros((nrec, nstep), jnp.float32)
    for n in range(nstep):
        records = compare(n, records)
    mis_ref[...] = records - obs_ref[...]

    def inject(n):
        def take(r, _):
            moved[pl.ds(r, 1), :] = rate[pl.ds(rec_ref[r], 1), :]
            return 0

        lax.fori_loop(0, nrec, take, 0, unroll=True)
        moved[...] = moved[...] + rec_rows[n]

        def put(r, _):
            rate[pl.ds(rec_ref[r], 1), :] = moved[pl.ds(r, 1), :]
            return 0

        lax.fori_loop(0, nrec, put, 0, unroll=True)

    def clear(at):
        rate[pl.ds(at, 16), :] = jnp.zeros((16, LANES), jnp.float32)

    rows16(clear)
    inject(nstep - 1)

    def last(at):
        value = rate[pl.ds(at, 16), :]
        field_a[pl.ds(edge + at, 16), :] = value
        dense[pl.ds(at, 16), :] = hist[(nstep - 1) % 2][(nstep - 1) // 2, pl.ds(at, 16), :] * value
        keep(0, at, value)

    rows16(last)
    multiply(0, 0, taps_a)

    def backward(n, of):
        inject(n - 1)

        def update(at, here, lap):
            here_rate = rate[pl.ds(at, 16), :] + speed[pl.ds(at, 16), :] * lap
            value = here + here_rate
            rate[pl.ds(at, 16), :] = here_rate
            fields[1 - of][pl.ds(edge + at, 16), :] = value
            dense[pl.ds(at, 16), :] = dense[pl.ds(at, 16), :] + hist[(nstep + of) % 2][(n - 1) // 2, pl.ds(at, 16), :] * here_rate
            keep(1 - of, at, value)

        sweep(of, update)

    def backward_pair(k, _):
        backward(nstep - 1 - 2 * k, 0)
        backward(nstep - 2 - 2 * k, 1)
        return 0

    lax.fori_loop(0, (nstep - 2) // 2, backward_pair, 0)
    if nstep % 2 == 1:
        backward(2, 0)
    end = fields[nstep % 2]

    def finish(at):
        image = dense[pl.ds(at, 16), :] - hist_a[0, pl.ds(at, 16), :] * end[pl.ds(edge + at, 16), :]
        dense[pl.ds(at, 16), :] = (2.0 / region[pl.ds(at, 16), :]) * image

    for r in range(held):
        @pl.when(give_ref[r] >= 0)
        def _():
            for j in range(0, slab, 16):
                finish(pl.multiple_of(give_ref[r] * slab + j, 16))
            give(r).start()

    for r in range(held):
        blank(r).wait()


def shot(aper, targets, take, give, rec_at, wavelet, pieces, sources, picks, same, observed):
    shape = pieces[0].shape
    slab = shape[1] * shape[2]
    ny, nz = shape[2:]
    cells = aper * slab
    held = give.shape[0]
    nstep, nrec = wavelet.shape[0], rec_at.shape[0]
    in_y = band(ny, CENTER_Y)
    none = np.zeros_like(in_y)
    mat_y = np.block([[in_y, in_y, none, none], [none, none, in_y, in_y]])
    in_z = band(nz, CENTER_Z)
    mat_z = np.concatenate([in_z, in_z], axis=0)
    smem = pl.BlockSpec(memory_space=pltpu.SMEM)
    vmem = pl.BlockSpec(memory_space=pltpu.VMEM)
    hbm = pl.BlockSpec(memory_space=pl.ANY)
    f32 = jnp.float32
    edge = REACH * ny
    *grads, misfit = pl.pallas_call(
        functools.partial(kernel, len(pieces), targets),
        out_shape=(
            *[jax.ShapeDtypeStruct((held // targets, slab, nz), f32)] * targets,
            jax.ShapeDtypeStruct((nrec, nstep), f32),
        ),
        in_specs=[smem] * 4 + [hbm] + [vmem] * 5 + [hbm] * len(pieces),
        out_specs=(*[hbm] * targets, vmem),
        scratch_shapes=[
            pltpu.VMEM(((nstep + 1) // 2, cells, nz), f32),
            pltpu.VMEM((nstep // 2, cells, nz), f32),
            pltpu.VMEM((cells + 2 * edge, nz), f32),
            pltpu.VMEM((cells + 2 * edge, nz), f32),
            pltpu.VMEM((cells, 2 * nz), jnp.bfloat16),
            pltpu.VMEM((cells, 2 * nz), jnp.bfloat16),
            pltpu.VMEM((GROUP * ny, nz), f32),
            pltpu.VMEM((GROUP * ny, nz), f32),
            pltpu.VMEM((cells, nz), f32),
            pltpu.VMEM((cells, nz), f32),
            pltpu.VMEM((cells, nz), f32),
            pltpu.VMEM((cells, nz), f32),
            pltpu.VMEM((nstep, nrec, nz), f32),
            pltpu.VMEM((nrec, nz), f32),
            pltpu.SemaphoreType.DMA((aper,)),
            pltpu.SemaphoreType.DMA,
            pltpu.SemaphoreType.DMA((held,)),
        ],
        compiler_params=pltpu.CompilerParams(vmem_limit_bytes=60 * 1024 * 1024),
        name="shot_gradient",
    )(
        take, give, rec_at, wavelet, sources, picks, same, observed,
        jnp.asarray(mat_y, jnp.bfloat16), jnp.asarray(mat_z, jnp.bfloat16),
        *[piece.reshape(-1, slab, nz) for piece in pieces],
    )
    return grads, misfit


SIDE_Z, SIDE_Y, SIDE_CORE = 4, 2, 2
Z_ORDER = (0, 2, 1, 3)


def place(z, y, core):
    return (z * SIDE_Y + y) * SIDE_CORE + core


def trade(block, z=0, y=0, core=0):
    flip = place(z, y, core)
    return lax.ppermute(block, "shot", [(i, i ^ flip) for i in range(SIDE_Z * SIDE_Y * SIDE_CORE)])


def collect(velocity):
    first, second = velocity[:1], velocity[1:]
    beside = trade(second, y=1)
    first = jnp.concatenate([first, trade(first, z=2)])
    second = jnp.concatenate([second, beside])
    second = jnp.concatenate([second, trade(second, z=2)])
    first = jnp.concatenate([first, trade(first, z=1)])
    pieces = [first, second, trade(first, y=1), trade(second, z=1)]
    return pieces + [trade(piece, core=1) for piece in pieces]


def collected():
    offsets = []
    for core in range(SIDE_CORE):
        offsets += [(place(a, 0, core), 0) for a in Z_ORDER]
        offsets += [(place(a, b, core), 1) for a in Z_ORDER[:2] for b in range(SIDE_Y)]
        offsets += [(place(a, 1, core), 0) for a in Z_ORDER]
        offsets += [(place(a, b, core), 1) for a in Z_ORDER[2:] for b in range(SIDE_Y)]
    return offsets


def handed():
    offsets = []
    for core in range(SIDE_CORE):
        offsets += [(place(a, b, core), 0) for b in range(SIDE_Y) for a in Z_ORDER]
        offsets += [(place(a, b, core), 1) for a in Z_ORDER for b in range(SIDE_Y)]
    return offsets


def reduce(grads):
    first, second, far_first, far_second = grads
    first = first + trade(far_first, core=1)
    second = second + trade(far_second, core=1)
    first, second = first[:4] + trade(first[4:], y=1), second[:4] + trade(second[4:], z=1)
    first, second = first[:2] + trade(first[2:], z=1), second[:2] + trade(second[2:], z=2)
    first, second = first[:1] + trade(first[1:], z=2), second[:1] + trade(second[1:], y=1)
    return jnp.concatenate([first, second])


def shards(velocity, tile_owner, aperture, source_at, source_amp, receivers, wavelet, observed):
    devices = lax.axis_size("shot")
    me = lax.axis_index("shot")
    per_dev = velocity.shape[0]
    slabs = aperture[0]
    aper = slabs.shape[0]
    nz = velocity.shape[3]
    store_rows = tile_owner[slabs] * per_dev + slabs // devices
    split = devices == SIDE_Z * SIDE_Y * SIDE_CORE and per_dev == 2
    if split:
        pieces = collect(velocity)
        taken, given = collected(), handed()
        outs = 2 * SIDE_CORE
    else:
        pieces = [lax.all_gather(velocity, "shot", axis=0, tiled=True)]
        taken = given = [(d, r) for d in range(devices) for r in range(per_dev)]
        me = 0
        outs = 1

    def slots(offsets):
        at = np.asarray(offsets, np.int32)
        rows = (me ^ at[:, 0]) * per_dev + at[:, 1]
        hit = rows[:, None] == store_rows[None, :]
        return jnp.max(jnp.where(hit, jnp.arange(aper, dtype=jnp.int32)[None, :], -1), axis=1)

    cells = aper * velocity.shape[1] * velocity.shape[2]
    sources = jnp.zeros((cells * nz,), jnp.float32).at[source_at[0]].add(source_amp[0]).reshape(cells, nz)
    rec_at = receivers[0] // nz
    lane = receivers[0] % nz
    picks = (lane[:, None] == jnp.arange(nz, dtype=jnp.int32)[None, :]).astype(jnp.float32)
    same = (rec_at[:, None] == rec_at[None, :]).astype(jnp.float32)
    grads, misfit = shot(
        aper, outs, slots(taken), slots(given), rec_at, wavelet, pieces, sources, picks, same, observed[0].T
    )
    if split:
        gradient = reduce(grads)
    else:
        gradient = lax.psum_scatter(grads[0], "shot", scatter_dimension=0, tiled=True)
    return (gradient.reshape(velocity.shape), misfit.T[None])


def solution(mesh):
    in_specs = (
        P(("groups", "shot"), None, None, None),
        P(),
        P(("groups", "shot"), None),
        P(("groups", "shot"), None),
        P(("groups", "shot"), None),
        P(("groups", "shot"), None),
        P(),
        P(("groups", "shot"), None, None),
    )
    out_specs = (P(("groups", "shot"), None, None, None), P(("groups", "shot"), None, None))
    return jax.shard_map(shards, mesh=mesh, in_specs=in_specs, out_specs=out_specs, check_vma=False)
```
